32 devices in a mesh: row: 4 (over y, core), col: 8 (over z, x).
Axes of the slice: x: 2, y: 2, z: 4, core: 2. Of those that a mesh axis runs over, the one named last changes fastest.
Arguments:
- child_fronts: float32 [20, 512, 20, 1024], P(None, 'col', None, 'row'), as said below
- parent_diagonal: float32 [16384], replicated, may hold values from 0.5 to 4
- block_maps: int32 [2, 20], replicated, may hold values from 0 to 31, as said below
Outputs:
- factored: float32 [16384, 16384], P('row', 'col')
The draws below stay inside these ranges and needn't reach their ends.
Inputs may be any that keep to these rules, and one draw needn't show every extreme that they name: `child_fronts`: each child's matrix is symmetric and positive definite. `block_maps`: each row names 20 distinct front blocks in increasing order; every one of the 32 front blocks is named by at least one row, and exactly 8 of them by both rows.
All inputs are finite; a program needn't handle non-finite values.
Results may differ from the reference program's by a relative error of at most 0.0001.
Values sent between devices are 32-bit elements; how exact they have to be, the bound alone decides.
A program may use at most 320 MiB of HBM per device.

```python
import math
import jax
import jax.numpy as jnp
from jax import lax

B = 512
F = 16384
NC = 10240
NB = 32
NCB = 20
N_ROW = 4
N_COL = 8


length_scale = 0.15


nugget_level = 1.0


def draw_child_fronts(key, part):
    matrices = []
    for which_child in range(2):
        subkey = jax.random.fold_in(key, 11 + which_child)
        point_key, scale_key = jax.random.split(subkey)
        points = jax.random.uniform(point_key, (NC, 3), jnp.float32)
        scales = jnp.exp(jax.random.uniform(scale_key, (NC,), jnp.float32, jnp.log(0.5), jnp.log(5.0)))
        squared = jnp.zeros((NC, NC), jnp.float32)
        for coord in range(3):
            spread = points[:, None, coord] - points[None, :, coord]
            squared = squared + spread * spread
        kernel = jnp.exp(-jnp.sqrt(squared) / length_scale)
        positions = jnp.arange(NC, dtype=jnp.int32)
        kernel = kernel + jnp.where(positions[:, None] == positions[None, :], nugget_level, 0.0)
        roots = jnp.sqrt(scales)
        matrix = roots[:, None] * kernel * roots[None, :]
        matrices.append(matrix.reshape(NCB, B, NCB, B))
    return jnp.concatenate(matrices, axis=3).astype(jnp.float32)


def draw_block_maps(key, part):
    shuffled = jax.random.permutation(jax.random.fold_in(key, 5), NB).astype(jnp.int32)
    first_map = jnp.sort(shuffled[:NCB])
    second_map = jnp.sort(shuffled[NB - NCB:])
    return jnp.stack([first_map, second_map], axis=0).astype(jnp.int32)


def setup_inputs(seed: int = 0) -> dict:
    seeds = jax.random.split(jax.random.key(seed), 4)
    child_fronts = draw_child_fronts(jax.random.fold_in(seeds[3], 71), 0)
    parent_diagonal = jnp.clip(jnp.exp(jax.random.uniform(seeds[1], (F,), jnp.float32, math.log(0.5), math.log(4.0))), 0.5, 4.0)
    block_maps = draw_block_maps(jax.random.fold_in(seeds[3], 71), 0)
    return dict(child_fronts=child_fronts, parent_diagonal=parent_diagonal, block_maps=block_maps)


def reference(child_fronts, parent_diagonal, block_maps):
    order_full = NB * B
    assembled = jnp.zeros((NB, NB, B, B), jnp.float32)
    for which_child in range(2):
        child_block = child_fronts[:, :, :, which_child * B:(which_child + 1) * B]
        child_block = jnp.transpose(child_block, (0, 2, 1, 3))
        placing = block_maps[which_child].astype(jnp.int32)
        assembled = assembled.at[placing[:, None], placing[None, :]].add(child_block)
    frontal = jnp.transpose(assembled, (0, 2, 1, 3)).reshape(order_full, order_full)
    indices = jnp.arange(order_full, dtype=jnp.int32)
    frontal = frontal.at[indices, indices].add(parent_diagonal)
    for panel_index in range(2):
        start_row = panel_index * B
        stop_row = start_row + B
        factor_block = jnp.linalg.cholesky(frontal[start_row:stop_row, start_row:stop_row])
        below_rows = frontal[stop_row:, start_row:stop_row]
        solved = jax.scipy.linalg.solve_triangular(factor_block, below_rows.T, lower=True).T
        trailing = frontal[stop_row:, stop_row:] - jnp.dot(solved.astype(jnp.float32), solved.T.astype(jnp.float32), precision=lax.Precision.HIGHEST, preferred_element_type=jnp.float32)
        frontal = frontal.at[stop_row:, stop_row:].set(trailing)
        frontal = frontal.at[start_row:stop_row, start_row:stop_row].set(factor_block)
        frontal = frontal.at[stop_row:, start_row:stop_row].set(solved)
        frontal = frontal.at[:start_row, start_row:stop_row].set(0.0)
        frontal = frontal.at[start_row:stop_row, stop_row:].set(0.0)
    shaped = frontal.reshape(NB // N_ROW, N_ROW, B, NB // N_COL, N_COL, B)
    shaped = jnp.transpose(shaped, (1, 0, 2, 4, 3, 5))
    return shaped.reshape(order_full, order_full)
```

```python
import functools

import jax
import jax.numpy as jnp
from jax import lax
from jax.experimental import pallas as pl
from jax.experimental.pallas import tpu as pltpu
from jax.sharding import PartitionSpec as P

B = 512
VMEM_LIMIT = 48 * 1024 * 1024


def inverse_maps(block_maps, count):
    blocks = jnp.arange(count, dtype=jnp.int32)
    matches = block_maps[:, None, :] == blocks[None, :, None]
    present = jnp.any(matches, axis=2)
    places = jnp.arange(block_maps.shape[1], dtype=jnp.int32)
    source = jnp.sum(jnp.where(matches, places[None, None, :], 0), axis=2)
    return (source.astype(jnp.int32), present)


def combine_kernel(blocks, chunk, source_ref, present_ref, rows_ref, a_ref, b_ref, o_ref):
    J = pl.program_id(0)
    for m in range(chunk):
        keep_a = present_ref[J] * rows_ref[m] > 0
        keep_b = present_ref[blocks + J] * rows_ref[chunk + m] > 0
        o_ref[0, m, 0] = jnp.where(keep_a, a_ref[0, :, m, 0], 0.0) + jnp.where(
            keep_b, b_ref[0, :, m, 0], 0.0
        )


def combine(received, source, present, rows_present, column_count):
    _, half_count, chunk, _, slice_rows, slice_cols = received.shape
    blocks = source.shape[1]
    local_cols = blocks // column_count

    def child_block(child):
        return pl.BlockSpec(
            (1, half_count, chunk, 1, slice_rows, slice_cols),
            lambda J, source, present, rows: (child, 0, 0, source[child * blocks + J], 0, 0),
        )

    return pl.pallas_call(
        functools.partial(combine_kernel, blocks, chunk),
        grid_spec=pltpu.PrefetchScalarGridSpec(
            num_scalar_prefetch=3,
            grid=(blocks,),
            in_specs=[child_block(0), child_block(1)],
            out_specs=pl.BlockSpec(
                (1, chunk, 1, half_count, slice_rows, slice_cols),
                lambda J, source, present, rows: (
                    lax.rem(J, column_count), 0, lax.div(J, column_count), 0, 0, 0
                ),
            ),
        ),
        out_shape=jax.ShapeDtypeStruct(
            (column_count, chunk, local_cols, half_count, slice_rows, slice_cols), jnp.float32
        ),
        compiler_params=pltpu.CompilerParams(vmem_limit_bytes=VMEM_LIMIT),
        cost_estimate=pl.CostEstimate(
            flops=received.size, bytes_accessed=12 * received.size, transcendentals=0
        ),
    )(
        source.reshape(-1),
        present.astype(jnp.int32).reshape(-1),
        rows_present.astype(jnp.int32).reshape(-1),
        received,
        received,
    )


def split(x):
    high = x.astype(jnp.bfloat16)
    low = (x - high.astype(jnp.float32)).astype(jnp.bfloat16)
    return high, low


def update_kernel(first, row_count, column_count, place_ref, *refs):
    piece_ref, diag_ref, left_ref, right_ref, o_ref = refs[-5:]
    I = place_ref[0] + row_count * (first + pl.program_id(0))
    J = place_ref[1] + column_count * pl.program_id(1)
    _, _, _, half_count, slice_rows, slice_cols = piece_ref.shape

    @pl.when((I < 2) & (J >= 2))
    def _():
        o_ref[...] = jnp.zeros_like(o_ref)

    for k in range(2):
        @pl.when(J == k)
        def _():
            o_ref[...] = left_ref[:, 0, :, k * B : (k + 1) * B].reshape(B, B)

    @pl.when((I >= 2) & (J >= 2))
    def _():
        dims = (((1,), (1,)), ((), ()))
        dot = functools.partial(
            lax.dot_general, dimension_numbers=dims, preferred_element_type=jnp.float32
        )
        left_high, left_low = split(left_ref[:, 0].reshape(B, 2 * B))
        right_high, right_low = split(right_ref[:, 0].reshape(B, 2 * B))
        product = dot(left_high, right_low) + dot(left_low, right_high)
        product = product + dot(left_high, right_high)
        for h in range(half_count):
            columns = slice(h * slice_cols, (h + 1) * slice_cols)
            part = piece_ref[:, 0, 0, h].reshape(B, slice_cols)
            o_ref[:, columns] = part - product[:, columns]

    @pl.when((I == J) & (I >= 2))
    def _():
        same = lax.broadcasted_iota(jnp.int32, (B, B), 0) == lax.broadcasted_iota(
            jnp.int32, (B, B), 1
        )
        o_ref[...] += jnp.where(same, diag_ref[0], 0.0)


def update(previous, pieces, diag_table, left, right, place, first, local_rows, row_count):
    column_count, chunk, local_cols, half_count, slice_rows, slice_cols = pieces.shape
    aliased = previous is not None
    in_specs = [
        pl.BlockSpec(
            (column_count, 1, 1, half_count, slice_rows, slice_cols),
            lambda m, n, place: (0, m, n, 0, 0, 0),
        ),
        pl.BlockSpec(
            (1, 1, B), lambda m, n, place: (place[0] + row_count * (first + m), 0, 0)
        ),
        pl.BlockSpec(
            (column_count, 1, slice_rows, 2 * B), lambda m, n, place: (0, first + m, 0, 0)
        ),
        pl.BlockSpec((column_count, 1, slice_rows, 2 * B), lambda m, n, place: (0, n, 0, 0)),
    ]
    operands = [pieces, diag_table, left, right]
    if aliased:
        in_specs = [pl.BlockSpec(memory_space=pl.ANY)] + in_specs
        operands = [previous] + operands
    size = chunk * local_cols * B * B
    return pl.pallas_call(
        functools.partial(update_kernel, first, row_count, column_count),
        grid_spec=pltpu.PrefetchScalarGridSpec(
            num_scalar_prefetch=1,
            grid=(chunk, local_cols),
            in_specs=in_specs,
            out_specs=pl.BlockSpec((B, B), lambda m, n, place: (first + m, n)),
        ),
        out_shape=jax.ShapeDtypeStruct((local_rows * B, local_cols * B), jnp.float32),
        input_output_aliases={1: 0} if aliased else {},
        compiler_params=pltpu.CompilerParams(vmem_limit_bytes=VMEM_LIMIT),
        cost_estimate=pl.CostEstimate(
            flops=size * 12 * B, bytes_accessed=16 * size, transcendentals=0
        ),
    )(place, *operands)


def shards(child_fronts, parent_diagonal, block_maps):
    row_count = lax.axis_size("row")
    column_count = lax.axis_size("col")
    row_index = lax.axis_index("row")
    column_index = lax.axis_index("col")
    half_count = row_count // 2
    blocks = parent_diagonal.shape[0] // B
    local_rows = blocks // row_count
    local_cols = blocks // column_count
    slice_rows = B // column_count
    slice_cols = 2 * B // row_count
    child_blocks = block_maps.shape[1]
    source, present = inverse_maps(block_maps, blocks)
    my_source = lax.dynamic_index_in_dim(source, row_index // half_count, 0, keepdims=False)
    row_blocks = jnp.arange(local_rows, dtype=jnp.int32) * row_count + row_index
    rows_present = jnp.take(present, row_blocks, axis=1, mode="clip")
    by_owner = my_source.reshape(local_rows, row_count).T
    diag_table = parent_diagonal.reshape(blocks, 1, B)
    place = jnp.stack([row_index, column_index]).astype(jnp.int32)

    by_block = child_fronts.transpose(0, 2, 1, 3)

    panel = jnp.take(by_block, my_source[:2], axis=1, mode="clip")
    panel = jnp.take(panel, by_owner.reshape(-1), axis=0, mode="clip")
    panel = panel.reshape(row_count, local_rows, 2, slice_rows, slice_cols)
    panel = lax.all_to_all(panel, "row", split_axis=0, concat_axis=0, tiled=True)
    panel = panel.reshape(2, half_count, local_rows, 2, slice_rows, slice_cols)
    keep = rows_present[:, :, None] & present[:, None, :2]
    panel = jnp.where(keep[:, None, :, :, None, None], panel, 0.0)
    panel = (panel[0] + panel[1]).transpose(1, 3, 2, 0, 4)
    panel = panel.reshape(local_rows, slice_rows, 2 * B)
    positions = (
        row_blocks[:, None] * B
        + column_index * slice_rows
        + jnp.arange(slice_rows, dtype=jnp.int32)[None, :]
    )
    on_diagonal = positions[:, :, None] == jnp.arange(2 * B, dtype=jnp.int32)[None, None, :]
    panel = panel + jnp.where(on_diagonal, parent_diagonal[None, None, : 2 * B], 0.0)

    corner = lax.all_gather(panel[0], ("row", "col"), axis=0, tiled=False)
    corner = corner.reshape(row_count * B, 2 * B)[: 2 * B]
    lower = lax.linalg.cholesky(corner, symmetrize_input=False)
    solved = jax.scipy.linalg.solve_triangular(
        lower, panel.reshape(-1, 2 * B).T, lower=True
    ).T.reshape(local_rows, slice_rows, 2 * B)
    own = lax.dynamic_slice_in_dim(
        lower,
        jnp.minimum(row_index, 1) * B + column_index * slice_rows,
        slice_rows,
        axis=0,
    )
    solved = jnp.where((row_blocks < 2)[:, None, None], own[None], solved)
    left = lax.all_gather(solved, "col", axis=0, tiled=False)
    owner_rows = (
        jnp.arange(local_cols, dtype=jnp.int32) * column_count + column_index
    ) // row_count
    right = jnp.take(left, owner_rows, axis=1, mode="clip")
    mine = row_index == lax.rem(column_index, row_count)
    right = lax.psum(jnp.where(mine, right, 0.0), "row")

    chunks = min(4, local_rows)
    chunk = local_rows // chunks
    pieces = []
    for q in range(chunks):
        rows = slice(q * chunk, (q + 1) * chunk)
        buffer = jnp.take(by_block, by_owner[:, rows].reshape(-1), axis=0, mode="clip")
        buffer = buffer.reshape(row_count, chunk, child_blocks, slice_rows, slice_cols)
        received = lax.all_to_all(buffer, "row", split_axis=0, concat_axis=0, tiled=True)
        received = received.reshape(
            2, half_count, chunk, child_blocks, slice_rows, slice_cols
        )
        summed = combine(received, source, present, rows_present[:, rows], column_count)
        pieces.append(
            lax.all_to_all(summed, "col", split_axis=0, concat_axis=0, tiled=True)
        )
    result = None
    for q in range(chunks):
        result = update(
            result, pieces[q], diag_table, left, right, place, q * chunk, local_rows, row_count
        )
    return result


def solution(mesh):
    return jax.shard_map(
        shards,
        mesh=mesh,
        in_specs=(P(None, "col", None, "row"), P(), P()),
        out_specs=P("row", "col"),
        check_vma=False,
    )
```
